512 devices in a mesh: leaf: 16 (over z), panel: 32 (over y, x, core).
Axes of the slice: x: 4, y: 4, z: 16, core: 2. Of those that a mesh axis runs over, the one named last changes fastest.
Arguments:
- probe_low: bfloat16 [16, 4096, 256], P('leaf', 'panel'), may hold values from -6 to 6
- probe_mid: bfloat16 [16, 2048, 256], P('leaf', 'panel'), may hold values from -6 to 6
- probe_top: bfloat16 [16, 1024, 256], P('leaf', 'panel'), may hold values from -6 to 6
- inv_low: bfloat16 [16, 4096, 4096], P('leaf', 'panel'), may hold values from -0.09375 to 0.09375
- inv_mid: bfloat16 [16, 2048, 4096], P('leaf', 'panel'), may hold values from -0.09375 to 0.09375
- inv_top: bfloat16 [16, 1024, 4096], P('leaf', 'panel'), may hold values from -0.09375 to 0.09375
- gram_low: bfloat16 [16, 4096, 4096], P('leaf', 'panel'), may hold values from -0.09375 to 0.09375
- gram_mid: bfloat16 [16, 2048, 4096], P('leaf', 'panel'), may hold values from -0.09375 to 0.09375
- gram_top: bfloat16 [16, 1024, 4096], P('leaf', 'panel'), may hold values from -0.09375 to 0.09375
- panel_low: bfloat16 [16, 1024, 4096], P('leaf', 'panel'), may hold values from -0.09375 to 0.09375
- panel_mid: bfloat16 [16, 512, 4096], P('leaf', 'panel'), may hold values from -0.09375 to 0.09375
- back_low: bfloat16 [16, 4096, 1024], P('leaf', 'panel'), may hold values from -0.1875 to 0.1875
- back_mid: bfloat16 [16, 2048, 1024], P('leaf', 'panel'), may hold values from -0.1875 to 0.1875
- sep_low: int32 [16, 1024], replicated, may hold values from 0 to 4095, as said below
- sep_mid: int32 [8, 1024], replicated, may hold values from 0 to 4095, as said below
Outputs:
- half_low: bfloat16 [16, 4096, 256], P('leaf', 'panel')
- half_mid: bfloat16 [16, 2048, 256], P('leaf', 'panel')
- half_top: bfloat16 [16, 1024, 256], P('leaf', 'panel')
- solved_low: bfloat16 [16, 4096, 256], P('leaf', 'panel')
- solved_mid: bfloat16 [16, 2048, 256], P('leaf', 'panel')
- solved_top: bfloat16 [16, 1024, 256], P('leaf', 'panel')
The draws below stay inside these ranges and needn't reach their ends.
Inputs may be any that keep to these rules, and one draw needn't show every extreme that they name: Each row of sep_low lists 1024 distinct rows of a parent supernode; 0 and 4095 occur in every row. Each row of sep_mid lists 1024 distinct rows of a parent supernode; 0 and 4095 occur in every row.
All inputs are finite; a program needn't handle non-finite values.
Results may differ from the reference program's by a relative error of at most 0.0085.
Values may be sent and summed in bfloat16 or wider, within the bound.
A program may use at most 64 MiB of HBM per device.

```python
import jax
import jax.numpy as jnp
from jax import lax

W = 4096
R = 1024
K = 256
LEAVES = 16


def separator_rows(key, count):
    keys = jax.random.split(key, count)

    def one_row(row_key):
        first_key, second_key = jax.random.split(row_key)
        inner = jax.random.permutation(first_key, W - 2)[:R - 2].astype(jnp.int32) + 1
        ends = jnp.array([0, W - 1], jnp.int32)
        joined = jnp.concatenate([ends, inner])
        return joined[jax.random.permutation(second_key, R)]
    return jax.vmap(one_row)(keys)


def draw_sep_low(key, part):
    return separator_rows(jax.random.fold_in(key, 11), LEAVES)


def draw_sep_mid(key, part):
    return separator_rows(jax.random.fold_in(key, 23), LEAVES // 2)


def steps_of(key, dims, pieces, low, largest):
    loudness, own = 1.0, jax.random.fold_in(key, 6)
    for dim, shards_of in pieces:
        steps = jnp.exp(jax.random.uniform(jax.random.fold_in(own, dim), (shards_of,), jnp.float32, low / len(pieces), largest / len(pieces)))
        loudness = loudness * jnp.repeat(steps, dims[dim] // shards_of).reshape([-1 if axis == dim else 1 for axis in range(len(dims))])
    return loudness


def scatter_about(stream_key, shape, spread, bound, pieces=(), kind=jnp.bfloat16):
    level = steps_of(stream_key, shape, pieces, -0.22, 0.18) if pieces else 1.0
    result = jax.random.normal(stream_key, shape, jnp.float32) * spread * level
    return jnp.minimum(jnp.maximum(result, -bound), bound).astype(kind)


def setup_inputs(seed: int = 0) -> dict:
    splits = jax.random.split(jax.random.key(seed), 16)
    return {
        "probe_low": scatter_about(splits[0], (LEAVES, W, K), 1.0, 6.0, ((0, 16), (1, 32))),
        "probe_mid": scatter_about(splits[1], (LEAVES, W // 2, K), 1.0, 6.0, ((0, 16), (1, 32))),
        "probe_top": scatter_about(splits[2], (LEAVES, W // 4, K), 1.0, 6.0, ((0, 16), (1, 32))),
        "inv_low": scatter_about(splits[3], (LEAVES, W, W), W ** -0.5, 0.09375, ((0, 16), (1, 32))),
        "inv_mid": scatter_about(splits[4], (LEAVES, W // 2, W), W ** -0.5, 0.09375, ((0, 16), (1, 32))),
        "inv_top": scatter_about(splits[5], (LEAVES, W // 4, W), W ** -0.5, 0.09375, ((0, 16), (1, 32))),
        "gram_low": scatter_about(splits[6], (LEAVES, W, W), W ** -0.5, 0.09375, ((0, 16), (1, 32))),
        "gram_mid": scatter_about(splits[7], (LEAVES, W // 2, W), W ** -0.5, 0.09375, ((0, 16), (1, 32))),
        "gram_top": scatter_about(splits[8], (LEAVES, W // 4, W), W ** -0.5, 0.09375, ((0, 16), (1, 32))),
        "panel_low": scatter_about(splits[9], (LEAVES, R, W), W ** -0.5, 0.09375, ((0, 16), (1, 32))),
        "panel_mid": scatter_about(splits[10], (LEAVES, R // 2, W), W ** -0.5, 0.09375, ((0, 16), (1, 32))),
        "back_low": scatter_about(splits[11], (LEAVES, W, R), R ** -0.5, 0.1875, ((0, 16), (1, 32))),
        "back_mid": scatter_about(splits[12], (LEAVES, W // 2, R), R ** -0.5, 0.1875, ((0, 16), (1, 32))),
        "sep_low": draw_sep_low(jax.random.fold_in(splits[15], 71), 0),
        "sep_mid": draw_sep_mid(jax.random.fold_in(splits[15], 71), 0),
    }


def per_block(mats, rhs):
    return lax.map(lambda pair: jnp.dot(pair[0], pair[1], preferred_element_type=jnp.float32), (mats, rhs))


def parent_side(updates, rows, probe):
    pairs = updates.reshape(probe.shape[0], 2, updates.shape[1], updates.shape[2])
    maps = rows.reshape(probe.shape[0], 2, rows.shape[1])

    def one_parent(item):
        upd, index_rows, own = item
        total = jnp.zeros(own.shape, jnp.float32)
        total = total.at[index_rows[0]].add(upd[0].astype(jnp.float32))
        total = total.at[index_rows[1]].add(upd[1].astype(jnp.float32))
        return (own.astype(jnp.float32) - total).astype(jnp.bfloat16)

    return lax.map(one_parent, (pairs, maps, probe))


def taken_rows(rows, parents):
    doubled = jnp.repeat(parents, 2, axis=0)
    return jax.vmap(lambda index_rows, block: jnp.take(block, index_rows, axis=0))(rows, doubled)


def reference(probe_low, probe_mid, probe_top, inv_low, inv_mid, inv_top, gram_low, gram_mid, gram_top, panel_low, panel_mid, back_low, back_mid, sep_low, sep_mid):
    leaves = probe_low.shape[0]

    def group(arr, level):
        return arr.reshape(leaves >> level, -1, arr.shape[-1])

    right_low = group(probe_low, 0)
    update_low = per_block(group(panel_low, 0), right_low).astype(jnp.bfloat16)
    right_mid = parent_side(update_low, sep_low, group(probe_mid, 1))
    update_mid = per_block(group(panel_mid, 1), right_mid).astype(jnp.bfloat16)
    right_top = parent_side(update_mid, sep_mid, group(probe_top, 2))
    half_low = per_block(group(inv_low, 0), right_low).astype(jnp.bfloat16)
    half_mid = per_block(group(inv_mid, 1), right_mid).astype(jnp.bfloat16)
    half_top = per_block(group(inv_top, 2), right_top).astype(jnp.bfloat16)
    solved_top = per_block(group(gram_top, 2), right_top).astype(jnp.bfloat16)
    taken_mid = taken_rows(sep_mid, solved_top)
    solved_mid = (per_block(group(gram_mid, 1), right_mid) - per_block(group(back_mid, 1), taken_mid)).astype(jnp.bfloat16)
    taken_low = taken_rows(sep_low, solved_mid)
    solved_low = (per_block(group(gram_low, 0), right_low) - per_block(group(back_low, 0), taken_low)).astype(jnp.bfloat16)
    return (half_low.reshape(probe_low.shape), half_mid.reshape(probe_mid.shape), half_top.reshape(probe_top.shape),
            solved_low.reshape(probe_low.shape), solved_mid.reshape(probe_mid.shape), solved_top.reshape(probe_top.shape))
```

```python
import jax
import jax.numpy as jnp
from jax import lax
from jax.experimental import pallas as pl
from jax.experimental.pallas import tpu as pltpu
from jax.sharding import PartitionSpec as P

MESH = pl.DeviceIdType.MESH
BF16, F32 = jnp.bfloat16, jnp.float32
HALF = 128
RIGHT_LOW, UPDATE_LOW, UPDATE_MID, SOLVED_TOP, SOLVED_MID, PROBE_MID, PROBE_TOP = range(7)


def kernel(
    probe_low, probe_mid, probe_top, inv_low, inv_mid, inv_top, gram_low, gram_mid, gram_top,
    panel_low, panel_mid, back_low, back_mid, sep_low, sep_mid,
    half_low, half_mid, half_top, solved_low, solved_mid, solved_top,
    d_rl, d_ul, d_um, d_st, d_sm, d_pm, d_pt,
    m_pl, m_low, m_mid, m_top, b_low, b_mid, s_low, s_mid, onehot, onehot_t, high,
    q_mid, q_top, c_low, c_mid, acc_low, acc_mid, acc_top,
    o_hl, o_hm, o_ht, o_sl, o_sm, o_st,
    load_sem, out_sem, core_send, core_recv, send_sem, recv_sem,
):
    z = lax.axis_index("leaf")
    p = lax.axis_index("panel")
    c = lax.rem(p, 2)
    x = lax.rem(p // 2, 4)
    y = p // 8
    z2, z4 = lax.rem(z, 2), lax.rem(z, 4)
    cols = pl.ds(pl.multiple_of(c * HALF, HALF), HALF)
    other_cols = pl.ds(pl.multiple_of((1 - c) * HALF, HALF), HALF)

    def chip(xx, yy):
        return {"leaf": z, "panel": (yy * 4 + xx) * 2 + c}

    sibling = {"leaf": z, "panel": p + 1 - 2 * c}

    loads = []

    def load(src, dst):
        copy = pltpu.make_async_copy(src, dst, load_sem.at[len(loads)])
        copy.start()
        loads.append(copy)
        return copy

    def rows(count):
        return pl.ds(pl.multiple_of(c * count, count), count)

    own = [
        load(probe_low.at[0, :, cols], d_rl.at[0, y, x, rows(128)]),
        load(probe_mid.at[0, :, cols], d_pm.at[z2, y, x, rows(64)]),
        load(probe_top.at[0, :, cols], d_pt.at[z4, y, x, rows(32)]),
    ]
    load_sep = [load(sep_low, s_low), load(sep_mid, s_mid)]
    load_pl = load(panel_low.at[0], m_pl.at[c])
    load_mid = [
        load(panel_mid.at[0], m_mid.at[c, 0:16]),
        load(inv_mid.at[0], m_mid.at[c, 16:80]),
        load(gram_mid.at[0], m_mid.at[c, 80:144]),
    ]
    load_low = [load(inv_low.at[0], m_low.at[c, 0]), load(gram_low.at[0], m_low.at[c, 1])]
    load_top = [load(gram_top.at[0], m_top.at[c, 0:32]), load(inv_top.at[0], m_top.at[c, 32:64])]
    load_back = [load(back_low.at[0], b_low), load(back_mid.at[0], b_mid)]

    barrier = pltpu.get_barrier_semaphore()
    pl.semaphore_signal(barrier, 1, device_id=sibling, device_id_type=MESH)
    for d in (1, 2, 3):
        pl.semaphore_signal(barrier, 1, device_id=chip(x ^ d, y), device_id_type=MESH)
        pl.semaphore_signal(barrier, 1, device_id=chip(x, y ^ d), device_id_type=MESH)
        pl.semaphore_signal(barrier, 1, device_id={"leaf": z ^ d, "panel": p}, device_id_type=MESH)
    pl.semaphore_wait(barrier, 10)

    sent = []

    core_count = [0]

    def swap(src, dst, arriving):
        i = core_count[0]
        core_count[0] += 1
        copy = pltpu.make_async_remote_copy(
            src, dst, core_send.at[i], core_recv.at[i], device_id=sibling, device_id_type=MESH
        )
        copy.start()
        sent.append(copy)
        return pltpu.make_async_remote_copy(
            arriving, arriving, core_send.at[i], core_recv.at[i], device_id=sibling, device_id_type=MESH
        )

    def other(count):
        return pl.ds(pl.multiple_of((1 - c) * count, count), count)

    def swap_probe(src, buf, zz, n):
        return swap(
            src.at[0, :, other_cols], buf.at[zz, y, x, rows(n)], buf.at[zz, y, x, other(n)]
        )

    in_rl = swap_probe(probe_low, d_rl, 0, 128)
    in_pm = swap_probe(probe_mid, d_pm, z2, 64)
    in_pt = swap_probe(probe_top, d_pt, z4, 32)

    def swap_rows(src, buf, *place):
        return swap(src, buf.at[(c, *place)], buf.at[(1 - c, *place)])

    in_pl = swap_rows(panel_low.at[0], m_pl)

    def z_copy(buf, g, size, d):
        zz = lax.rem(z, size)

        def make(at):
            return pltpu.make_async_remote_copy(
                buf.at[at, y, x], buf.at[at, y, x], send_sem.at[g, 0, d - 1], recv_sem.at[g, 0, d - 1],
                device_id={"leaf": z ^ d, "panel": p}, device_id_type=MESH,
            )

        return make(zz), make(zz ^ d)

    def first_copy(buf, g, d):
        xd = jnp.where(c == 0, x ^ d, x)
        yd = jnp.where(c == 0, y, y ^ d)

        def make(xx, yy):
            return pltpu.make_async_remote_copy(
                buf.at[:, yy, xx], buf.at[:, yy, xx], send_sem.at[g, 1, d - 1], recv_sem.at[g, 1, d - 1],
                device_id=chip(xd, yd), device_id_type=MESH,
            )

        return make(x, y), make(xd, yd)

    def second_row(buf, g, d):
        def make(yy):
            return pltpu.make_async_remote_copy(
                buf.at[:, yy], buf.at[:, yy], send_sem.at[g, 2, d - 1], recv_sem.at[g, 2, d - 1],
                device_id=chip(x, y ^ d), device_id_type=MESH,
            )

        return make(y), make(y ^ d)

    def second_column(buf, g, d):
        def make(xx):
            return pltpu.make_async_remote_copy(
                buf.at[:, :, xx], buf.at[:, :, xx], send_sem.at[g, 2, d - 1], recv_sem.at[g, 2, d - 1],
                device_id=chip(x ^ d, y), device_id_type=MESH,
            )

        return make(x), make(x ^ d)

    def z_start(buf, g, size):
        for d in range(1, size):
            z_copy(buf, g, size, d)[0].start()

    def z_wait(buf, g, size):
        for d in range(1, size):
            out, arriving = z_copy(buf, g, size, d)
            arriving.wait_recv()
            out.wait_send()

    def first_start(buf, g):
        for d in (1, 3, 2):
            first_copy(buf, g, d)[0].start()

    def first_wait(buf, g):
        for d in (1, 3, 2):
            out, arriving = first_copy(buf, g, d)
            arriving.wait_recv()
            out.wait_send()

    def second(act):
        @pl.when(c == 0)
        def _():
            for d in (1, 3, 2):
                act(second_row, d)

        @pl.when(c == 1)
        def _():
            for d in (1, 3, 2):
                act(second_column, d)

    def second_start(buf, g):
        second(lambda make, d: make(buf, g, d)[0].start())

    def second_wait(buf, g):
        def act(make, d):
            out, arriving = make(buf, g, d)
            arriving.wait_recv()
            out.wait_send()

        second(act)

    def dot(a, b):
        return jnp.dot(a, b, preferred_element_type=F32)

    def whole(buf):
        return buf[...].reshape(-1, HALF)

    def tables():
        for i in range(4):
            table, row = (s_low, (z - z2) + i) if i < 2 else (s_mid, 2 * (z // 4) + i - 2)
            sep = table[pl.ds(row, 1), :]
            high[i : i + 1, :] = lax.shift_right_logical(sep, 8)
            low = jnp.bitwise_and(sep, 255)
            for j in range(4):
                at = slice(j * 256, (j + 1) * 256)
                grid = lax.broadcasted_iota(jnp.int32, (256, 256), 0)
                hot = jnp.where(grid == low[:, at], 1.0, 0.0)
                onehot[i, :, at] = hot.astype(BF16)

    def own_tables():
        for i, (table, row) in enumerate(((s_low, z), (s_mid, z // 2))):
            sep = table[pl.ds(row, 1), :]
            high[4 + i : 5 + i, :] = lax.shift_right_logical(sep, 8)
            low = jnp.bitwise_and(sep, 255)
            for j in range(4):
                at = slice(j * 256, (j + 1) * 256)
                grid = lax.broadcasted_iota(jnp.int32, (256, 256), 0)
                hot = jnp.where(grid == low[:, at], 1.0, 0.0)
                onehot_t[i, at, :] = hot.T.astype(BF16)

    def take_columns(src, dst, i, total, block):
        at0 = (i % 2) * 1024

        def step(r, _):
            part = pl.ds(pl.multiple_of(r * block, block), block)
            value = src[c, part, :]
            tall = jnp.concatenate([value[:, k * 256 : (k + 1) * 256] for k in range(16)], 0)
            for j in range(4):
                at = slice(j * 256, (j + 1) * 256)
                found = dot(tall, onehot[i, :, at])
                which = high[i : i + 1, at]
                picked = jnp.zeros((block, 256), F32)
                for k in range(16):
                    picked = jnp.where(which == k, found[k * block : (k + 1) * block], picked)
                dst[c, part, at0 + j * 256 : at0 + (j + 1) * 256] = picked.astype(BF16)
            return 0

        lax.fori_loop(0, total // block, step, 0)

    def spread_columns(src, dst, i, total, block):
        def step(r, _):
            part = pl.ds(pl.multiple_of(r * block, block), block)
            value = src[part, :]
            which = high[4 + i : 5 + i, :]
            tall = jnp.concatenate(
                [value * jnp.where(which == k, 1.0, 0.0).astype(BF16) for k in range(16)], 0
            )
            found = dot(tall, onehot_t[i])
            for k in range(16):
                dst[c, part, k * 256 : (k + 1) * 256] = found[k * block : (k + 1) * block].astype(BF16)
            return 0

        lax.fori_loop(0, total // block, step, 0)

    outs = []

    def give(out, buf):
        i = len(outs)
        copy = pltpu.make_async_copy(buf.at[c], out.at[0, :, cols], out_sem.at[i])
        copy.start()
        outs.append((copy, swap(buf.at[1 - c], out.at[0, :, cols], out.at[0, :, other_cols])))

    in_mid = [
        swap_rows(panel_mid.at[0], m_mid, slice(0, 16)),
        swap_rows(inv_mid.at[0], m_mid, slice(16, 80)),
        swap_rows(gram_mid.at[0], m_mid, slice(80, 144)),
    ]
    own[0].wait()
    in_rl.wait_recv()
    first_start(d_rl, RIGHT_LOW)
    own[1].wait()
    in_pm.wait_recv()
    z_start(d_pm, PROBE_MID, 2)
    own[2].wait()
    in_pt.wait_recv()
    z_start(d_pt, PROBE_TOP, 4)
    in_low = [
        swap_rows(inv_low.at[0], m_low, 0),
        swap_rows(gram_low.at[0], m_low, 1),
    ]
    in_top = [
        swap_rows(gram_top.at[0], m_top, slice(0, 32)),
        swap_rows(inv_top.at[0], m_top, slice(32, 64)),
    ]
    for copy in load_sep:
        copy.wait()
    tables()
    first_wait(d_rl, RIGHT_LOW)
    second_start(d_rl, RIGHT_LOW)
    z_wait(d_pm, PROBE_MID, 2)
    first_start(d_pm, PROBE_MID)
    for copy in load_mid:
        copy.wait()
    take_columns(m_mid, q_mid, 0, 144, 48)
    take_columns(m_mid, q_mid, 1, 144, 48)
    in_q_mid = swap_rows(q_mid.at[c], q_mid)
    load_pl.wait()
    in_pl.wait_recv()
    second_wait(d_rl, RIGHT_LOW)
    update = dot(m_pl[...].reshape(64, 4096), whole(d_rl))
    d_ul[z2, y, x] = update.astype(BF16)
    z_start(d_ul, UPDATE_LOW, 2)
    first_wait(d_pm, PROBE_MID)
    second_start(d_pm, PROBE_MID)
    own_tables()
    z_wait(d_ul, UPDATE_LOW, 2)
    first_start(d_ul, UPDATE_LOW)
    for copy in load_low:
        copy.wait()
    for copy in in_low:
        copy.wait_recv()
    result = dot(m_low[...].reshape(512, 4096), whole(d_rl)).reshape(2, 2, 128, HALF)
    o_hl[...] = result[:, 0].astype(BF16)
    acc_low[...] = result[:, 1]
    give(half_low, o_hl)
    first_wait(d_ul, UPDATE_LOW)
    second_start(d_ul, UPDATE_LOW)
    z_wait(d_pt, PROBE_TOP, 4)
    first_start(d_pt, PROBE_TOP)
    for copy in load_top:
        copy.wait()
    take_columns(m_top, q_top, 2, 64, 32)
    take_columns(m_top, q_top, 3, 64, 32)
    in_q_top = swap_rows(q_top.at[c], q_top)
    for copy in in_mid:
        copy.wait_recv()
    second_wait(d_pm, PROBE_MID)
    acc_mid[...] = dot(m_mid[...].reshape(288, 4096), whole(d_pm)).reshape(2, 144, HALF)
    in_q_mid.wait_recv()
    second_wait(d_ul, UPDATE_LOW)
    update = acc_mid[:, 0:16].reshape(32, HALF) - dot(q_mid[:, 0:16].reshape(32, 2048), whole(d_ul))
    d_um[z4, y, x] = update.astype(BF16)
    z_start(d_um, UPDATE_MID, 4)
    first_wait(d_pt, PROBE_TOP)
    second_start(d_pt, PROBE_TOP)
    result = acc_mid[:, 16:144] - dot(q_mid[:, 16:144].reshape(256, 2048), whole(d_ul)).reshape(2, 128, HALF)
    o_hm[...] = result[:, 0:64].astype(BF16)
    acc_mid[:, 16:144] = result
    give(half_mid, o_hm)
    z_wait(d_um, UPDATE_MID, 4)
    first_start(d_um, UPDATE_MID)
    for copy in load_back:
        copy.wait()
    spread_columns(b_mid, c_mid, 1, 64, 32)
    in_c_mid = swap_rows(c_mid.at[c], c_mid)
    first_wait(d_um, UPDATE_MID)
    second_start(d_um, UPDATE_MID)
    for copy in in_top:
        copy.wait_recv()
    second_wait(d_pt, PROBE_TOP)
    acc_top[...] = dot(m_top[...].reshape(128, 4096), whole(d_pt)).reshape(2, 64, HALF)
    in_q_top.wait_recv()
    second_wait(d_um, UPDATE_MID)
    result = acc_top[...] - dot(q_top[...].reshape(128, 2048), whole(d_um)).reshape(2, 64, HALF)
    top = result[:, 0:32].astype(BF16)
    d_st[z4, y, x] = top.reshape(64, HALF)
    z_start(d_st, SOLVED_TOP, 4)
    o_st[...] = top
    o_ht[...] = result[:, 32:64].astype(BF16)
    give(solved_top, o_st)
    give(half_top, o_ht)
    z_wait(d_st, SOLVED_TOP, 4)
    first_start(d_st, SOLVED_TOP)
    spread_columns(b_low, c_low, 0, 128, 32)
    in_c_low = swap_rows(c_low.at[c], c_low)
    first_wait(d_st, SOLVED_TOP)
    second_start(d_st, SOLVED_TOP)
    in_c_mid.wait_recv()
    second_wait(d_st, SOLVED_TOP)
    result = acc_mid[:, 80:144] - dot(c_mid[...].reshape(128, 4096), whole(d_st)).reshape(2, 64, HALF)
    mid = result.astype(BF16)
    d_sm[z2, y, x] = mid.reshape(128, HALF)
    z_start(d_sm, SOLVED_MID, 2)
    o_sm[...] = mid
    give(solved_mid, o_sm)
    z_wait(d_sm, SOLVED_MID, 2)
    first_start(d_sm, SOLVED_MID)
    first_wait(d_sm, SOLVED_MID)
    second_start(d_sm, SOLVED_MID)
    in_c_low.wait_recv()
    second_wait(d_sm, SOLVED_MID)
    result = acc_low[...] - dot(c_low[...].reshape(256, 4096), whole(d_sm)).reshape(2, 128, HALF)
    o_sl[...] = result.astype(BF16)
    give(solved_low, o_sl)
    for copy, arriving in outs:
        copy.wait()
        arriving.wait_recv()
    for copy in sent:
        copy.wait_send()


def body(*args):
    shapes = ((128, 0), (64, 1), (32, 2), (128, 0), (64, 1), (32, 2))

    def vmem(*shape, dtype=BF16):
        return pltpu.VMEM(shape, dtype)

    return pl.pallas_call(
        kernel,
        out_shape=tuple(jax.ShapeDtypeStruct((1, n, 256), BF16) for n, _ in shapes),
        in_specs=[pl.BlockSpec(memory_space=pl.ANY)] * 15,
        out_specs=tuple(pl.BlockSpec(memory_space=pl.ANY) for _ in shapes),
        scratch_shapes=[
            vmem(1, 4, 4, 256, HALF), vmem(2, 4, 4, 64, HALF), vmem(4, 4, 4, 32, HALF), vmem(4, 4, 4, 64, HALF),
            vmem(2, 4, 4, 128, HALF), vmem(2, 4, 4, 128, HALF), vmem(4, 4, 4, 64, HALF),
            vmem(2, 32, 4096), vmem(2, 2, 128, 4096), vmem(2, 144, 4096), vmem(2, 64, 4096),
            vmem(128, 1024), vmem(64, 1024),
            vmem(16, 1024, dtype=jnp.int32), vmem(8, 1024, dtype=jnp.int32),
            vmem(4, 256, 1024), vmem(2, 1024, 256), vmem(8, 1024, dtype=jnp.int32),
            vmem(2, 144, 2048), vmem(2, 64, 2048), vmem(2, 128, 4096), vmem(2, 64, 4096),
            vmem(2, 128, HALF, dtype=F32), vmem(2, 144, HALF, dtype=F32), vmem(2, 64, HALF, dtype=F32),
            vmem(2, 128, HALF), vmem(2, 64, HALF), vmem(2, 32, HALF),
            vmem(2, 128, HALF), vmem(2, 64, HALF), vmem(2, 32, HALF),
            pltpu.SemaphoreType.DMA((15,)), pltpu.SemaphoreType.DMA((6,)),
            pltpu.SemaphoreType.DMA((21,)), pltpu.SemaphoreType.DMA((21,)),
            pltpu.SemaphoreType.DMA((7, 3, 3)), pltpu.SemaphoreType.DMA((7, 3, 3)),
        ],
        compiler_params=pltpu.CompilerParams(
            collective_id=0, has_side_effects=True, vmem_limit_bytes=56 << 20
        ),
        cost_estimate=pl.CostEstimate(flops=7 * 10**9, bytes_accessed=10 << 20, transcendentals=0),
        name="sweeps",
    )(*args)


def solution(mesh):
    split = P("leaf", "panel", None)
    return jax.shard_map(
        body,
        mesh=mesh,
        in_specs=(split,) * 13 + (P(), P()),
        out_specs=(split,) * 6,
        check_vma=False,
    )
```

```python
import jax
import jax.numpy as jnp
from jax import lax
from jax.experimental import pallas as pl
from jax.experimental.pallas import tpu as pltpu
from jax.sharding import PartitionSpec as P

MESH = pl.DeviceIdType.MESH
BF16, F32 = jnp.bfloat16, jnp.float32
HALF = 128
COPIES = 192


def kernel(
    probe_low, probe_mid, probe_top, inv_low, inv_mid, inv_top, gram_low, gram_mid, gram_top,
    panel_low, panel_mid, back_low, back_mid, sep_low, sep_mid,
    half_low, half_mid, half_top, solved_low, solved_mid, solved_top,
    d_rl, d_ul, d_um, d_st, d_sm, d_pm, d_pt,
    m_pl, m_low, m_mid, m_top, b_low, b_mid, s_low, s_mid, onehot, onehot_t, high,
    q_mid, qg_top, qh_top, c_low, c_mid, acc_low, acc_mid, g_mid, pg_top, ph_top,
    o_hl, o_hm, o_ht, o_sl, o_sm, o_st,
    load_sem, out_sem, send_sem, recv_sem,
):
    z = lax.axis_index("leaf")
    p = lax.axis_index("panel")
    c = lax.rem(p, 2)
    x = lax.rem(p // 2, 4)
    y = p // 8
    z2, z4 = lax.rem(z, 2), lax.rem(z, 4)
    cols = pl.ds(pl.multiple_of(c * HALF, HALF), HALF)
    other_cols = pl.ds(pl.multiple_of((1 - c) * HALF, HALF), HALF)

    def place(d, e, core=c):
        return x ^ jnp.where(core == 0, d, e), y ^ jnp.where(core == 0, e, d)

    def device(d=0, e=0, dz=0, core=c):
        xx, yy = place(d, e, core)
        return {"leaf": z ^ dz, "panel": (yy * 4 + xx) * 2 + core}

    sibling = {"leaf": z, "panel": p + 1 - 2 * c}

    def rows(count):
        return pl.ds(pl.multiple_of(c * count, count), count)

    def other(count):
        return pl.ds(pl.multiple_of((1 - c) * count, count), count)

    n_loads = [0]

    def load(src, dst):
        copy = pltpu.make_async_copy(src, dst, load_sem.at[n_loads[0]])
        n_loads[0] += 1
        copy.start()
        return copy

    own = [
        load(probe_low.at[0, :, cols], d_rl.at[0, y, x, rows(128)]),
        load(probe_mid.at[0, :, cols], d_pm.at[z2, y, x, rows(64)]),
        load(probe_top.at[0, :, cols], d_pt.at[z4, y, x, rows(32)]),
    ]
    load_sep = [load(sep_low, s_low), load(sep_mid, s_mid)]
    load_mid = [
        load(panel_mid.at[0], m_mid.at[c, 0:16]),
        load(inv_mid.at[0], m_mid.at[c, 16:80]),
        load(gram_mid.at[0], m_mid.at[c, 80:144]),
    ]
    load_top = [load(gram_top.at[0], m_top.at[c, 0:32]), load(inv_top.at[0], m_top.at[c, 32:64])]
    load_pl = load(panel_low.at[0], m_pl.at[c])
    load_back = [load(back_low.at[0], b_low), load(back_mid.at[0], b_mid.at[z2])]
    load_low = [load(inv_low.at[0], m_low.at[c, 0]), load(gram_low.at[0], m_low.at[c, 1])]

    barrier = pltpu.get_barrier_semaphore()
    partners = [sibling]
    for d in (1, 2, 3):
        partners += [device(d), device(0, d), device(dz=d), device(d, dz=1)]
        partners += [device(d, core=1 - c), device(0, d, core=1 - c)]
    for partner in partners:
        pl.semaphore_signal(barrier, 1, device_id=partner, device_id_type=MESH)
    pl.semaphore_wait(barrier, len(partners))

    n_sent = [0]
    unsent = []

    def send(src, dst, to, arriving=None):
        i = n_sent[0]
        n_sent[0] += 1
        copy = pltpu.make_async_remote_copy(
            src, dst, send_sem.at[i], recv_sem.at[i], device_id=to, device_id_type=MESH
        )
        copy.start()
        unsent.append(copy)
        if arriving is None:
            arriving = dst

        def wait():
            pltpu.make_async_remote_copy(
                arriving, arriving, send_sem.at[i], recv_sem.at[i], device_id=to, device_id_type=MESH
            ).wait_recv()

        return wait

    def drain():
        for copy in unsent:
            copy.wait_send()
        unsent.clear()

    def all_of(waits):
        for wait in waits:
            wait()

    def swap(src, buf, *at):
        return send(src, buf.at[(c, *at)], sibling, buf.at[(1 - c, *at)])

    def swap_probe(src, buf, zz, n):
        return send(
            src.at[0, :, other_cols], buf.at[zz, y, x, rows(n)], sibling, buf.at[zz, y, x, other(n)]
        )

    class Gather:
        def __init__(self, buf):
            self.buf, self.first, self.second = buf, {1: [], 2: [], 3: [], 0: []}, []

        def part(self, d, e, zz=slice(None)):
            xx, yy = place(d, e)
            return self.buf.at[zz, yy, xx]

        def begin(self, zz=slice(None)):
            for d in (1, 3, 2):
                self.first[d].append(
                    send(self.part(0, 0, zz), self.part(0, 0, zz), device(d), self.part(d, 0, zz))
                )

        def begin_pair(self):
            here, there = z2, 1 - z2
            for d, dz in ((1, 0), (3, 0), (0, 1), (1, 1), (3, 1), (2, 0), (2, 1)):
                self.first[d].append(
                    send(
                        self.part(0, 0, here), self.part(0, 0, here), device(d, dz=dz),
                        self.part(d, 0, there if dz else here),
                    )
                )

        def planes(self, offsets, here):
            self.z = [
                (here ^ d, send(self.part(0, 0, here), self.part(0, 0, here), device(dz=d), self.part(0, 0, here ^ d)))
                for d in offsets
            ]

        def relay(self):
            for zz, wait in self.z:
                wait()
                for d in (1, 3, 2):
                    self.first[d].append(
                        send(self.part(0, 0, zz), self.part(0, 0, zz), device(d), self.part(d, 0, zz))
                    )

        def forward(self, *offsets):
            for d in offsets:
                all_of(self.first[d])
                for e in (1, 3, 2):
                    self.second.append(
                        send(self.part(d, 0), self.part(d, 0), device(0, e), self.part(d, e))
                    )

        def finish(self):
            all_of(self.second)

    def dot(a, b):
        return jnp.dot(a, b, preferred_element_type=F32)

    def whole(buf):
        return buf[...].reshape(-1, HALF)

    def tables(first, count):
        for i in range(first, first + count):
            table, row = (s_low, (z - z2) + i) if i < 2 else (s_mid, 2 * (z // 4) + i - 2)
            sep = table[pl.ds(row, 1), :]
            high[i : i + 1, :] = lax.shift_right_logical(sep, 8)
            low = jnp.bitwise_and(sep, 255)
            for j in range(4):
                at = slice(j * 256, (j + 1) * 256)
                grid = lax.broadcasted_iota(jnp.int32, (256, 256), 0)
                hot = jnp.where(grid == low[:, at], 1.0, 0.0)
                onehot[i, :, at] = hot.astype(BF16)

    def own_tables():
        for i, (table, row) in enumerate(((s_low, z), (s_mid, z // 2))):
            sep = table[pl.ds(row, 1), :]
            high[4 + i : 5 + i, :] = lax.shift_right_logical(sep, 8)
            low = jnp.bitwise_and(sep, 255)
            for j in range(4):
                at = slice(j * 256, (j + 1) * 256)
                grid = lax.broadcasted_iota(jnp.int32, (256, 256), 0)
                hot = jnp.where(grid == low[:, at], 1.0, 0.0)
                onehot_t[i, at, :] = hot.T.astype(BF16)

    def take_columns(src, start, dst, i, total, block):
        at0 = (i % 2) * 1024

        def step(r, _):
            value = src[c, pl.ds(pl.multiple_of(start + r * block, 16), block), :]
            tall = jnp.concatenate([value[:, k * 256 : (k + 1) * 256] for k in range(16)], 0)
            part = pl.ds(pl.multiple_of(r * block, 16), block)
            for j in range(4):
                at = slice(j * 256, (j + 1) * 256)
                found = dot(tall, onehot[i, :, at])
                which = high[i : i + 1, at]
                picked = jnp.zeros((block, 256), F32)
                for k in range(16):
                    picked = jnp.where(which == k, found[k * block : (k + 1) * block], picked)
                dst[part, at0 + j * 256 : at0 + (j + 1) * 256] = picked.astype(BF16)
            return 0

        lax.fori_loop(0, total // block, step, 0)

    def spread_columns(src, dst, i, total, block):
        def step(r, _):
            part = pl.ds(pl.multiple_of(r * block, block), block)
            value = src[part, :]
            which = high[4 + i : 5 + i, :]
            tall = jnp.concatenate(
                [value * jnp.where(which == k, 1.0, 0.0).astype(BF16) for k in range(16)], 0
            )
            found = dot(tall, onehot_t[i])
            for k in range(16):
                dst[part, k * 256 : (k + 1) * 256] = found[k * block : (k + 1) * block].astype(BF16)
            return 0

        lax.fori_loop(0, total // block, step, 0)

    given = []

    def give(out, buf):
        copy = pltpu.make_async_copy(buf.at[c], out.at[0, :, cols], out_sem.at[len(given)])
        copy.start()
        given.append((copy, send(buf.at[1 - c], out.at[0, :, cols], sibling, out.at[0, :, other_cols])))

    right_low = Gather(d_rl)
    mine = d_rl.at[0, y, x, rows(128)]
    for d in (1, 3, 2):
        xx, yy = place(d, 0)
        right_low.first[d].append(
            send(probe_low.at[0, :, cols], mine, device(d), d_rl.at[0, yy, xx, rows(128)])
        )
        right_low.first[d].append(
            send(probe_low.at[0, :, other_cols], mine, device(d, core=1 - c), d_rl.at[0, yy, xx, other(128)])
        )
    right_low.first[0].append(swap_probe(probe_low, d_rl, 0, 128))
    in_pm = swap_probe(probe_mid, d_pm, z2, 64)
    in_pt = swap_probe(probe_top, d_pt, z4, 32)
    in_back = send(back_mid.at[0], b_mid.at[z2], device(dz=1), b_mid.at[1 - z2])
    own[1].wait()
    in_pm()
    pm = Gather(d_pm)
    pm.planes((1,), z2)
    pm.begin(z2)
    own[2].wait()
    in_pt()
    pt = Gather(d_pt)
    pt.planes((1, 2, 3), z4)
    own[0].wait()
    right_low.forward(0)
    in_pl = swap(panel_low.at[0], m_pl)
    all_of([copy.wait for copy in load_sep])
    tables(2, 2)
    all_of([copy.wait for copy in load_top])
    take_columns(m_top, 0, qg_top.at[z4, c], 2, 32, 32)
    take_columns(m_top, 0, qg_top.at[z4, c], 3, 32, 32)
    piece = qg_top.at[z4, c]
    z_qg = [(d, send(piece, piece, device(dz=d), qg_top.at[z4 ^ d, c])) for d in (1, 2, 3)]
    right_low.forward(1, 3)
    pm.relay()
    right_low.forward(2)
    in_qg = [send(piece, piece, sibling, qg_top.at[z4, 1 - c])]
    in_mid = [
        swap(panel_mid.at[0], m_mid, slice(0, 16)),
        swap(inv_mid.at[0], m_mid, slice(16, 80)),
        swap(gram_mid.at[0], m_mid, slice(80, 144)),
    ]
    in_low = [swap(inv_low.at[0], m_low, 0), swap(gram_low.at[0], m_low, 1)]
    in_top = [swap(gram_top.at[0], m_top, slice(0, 32)), swap(inv_top.at[0], m_top, slice(32, 64))]
    tables(0, 2)
    all_of([copy.wait for copy in load_mid])
    take_columns(m_mid, 0, q_mid.at[c], 0, 144, 48)
    take_columns(m_mid, 0, q_mid.at[c], 1, 144, 48)
    in_q_mid = swap(q_mid.at[c], q_mid)
    pm.forward(0, 1, 3, 2)
    load_pl.wait()
    in_pl()
    right_low.finish()
    d_ul[z2, y, x] = dot(m_pl[...].reshape(64, 4096), whole(d_rl)).astype(BF16)

    update_low = Gather(d_ul)
    update_low.begin_pair()
    pt.begin(z4)
    pt.relay()
    own_tables()
    all_of([copy.wait for copy in load_back])
    in_back()
    spread_columns(b_mid.at[z2], c_mid.at[z2, c], 1, 64, 32)
    update_low.forward(0, 1, 3, 2)
    pt.forward(0, 1, 3, 2)
    spread_columns(b_mid.at[1 - z2], c_mid.at[1 - z2, c], 1, 64, 32)
    in_c_mid = [
        send(c_mid.at[zz, c], c_mid.at[zz, c], sibling, c_mid.at[zz, 1 - c]) for zz in (0, 1)
    ]
    drain()
    all_of(in_mid)
    pm.finish()
    acc_mid[...] = dot(m_mid[...].reshape(288, 4096), whole(d_pm)).reshape(2, 144, HALF)
    in_q_mid()
    update_low.finish()
    update = acc_mid[:, 0:16].reshape(32, HALF) - dot(q_mid[:, 0:16].reshape(32, 2048), whole(d_ul))
    d_um[z4, y, x] = update.astype(BF16)

    update_mid = Gather(d_um)
    update_mid.planes((1, 2, 3), z4)
    update_mid.begin(z4)
    result = acc_mid[:, 16:144] - dot(q_mid[:, 16:144].reshape(256, 2048), whole(d_ul)).reshape(2, 128, HALF)
    o_hm[...] = result[:, 0:64].astype(BF16)
    g_mid[z2] = result[:, 64:128]
    update_mid.relay()
    in_g_mid = send(g_mid.at[z2], g_mid.at[z2], device(dz=1), g_mid.at[1 - z2])
    give(half_mid, o_hm)
    for d, wait in z_qg:
        wait()
        piece = qg_top.at[z4 ^ d, c]
        in_qg.append(send(piece, piece, sibling, qg_top.at[z4 ^ d, 1 - c]))
    all_of([copy.wait for copy in load_low])
    all_of(in_low)
    result = dot(m_low[...].reshape(512, 4096), whole(d_rl)).reshape(2, 2, 128, HALF)
    o_hl[...] = result[:, 0].astype(BF16)
    acc_low[...] = result[:, 1]
    update_mid.forward(0, 1, 3, 2)
    give(half_low, o_hl)
    all_of(in_top)
    pt.finish()
    result = dot(m_top[...].reshape(128, 4096), whole(d_pt)).reshape(2, 64, HALF)
    pg_top[z4] = result[:, 0:32]
    ph_top[...] = result[:, 32:64]
    in_pg = [send(pg_top.at[z4], pg_top.at[z4], device(dz=d), pg_top.at[z4 ^ d]) for d in (1, 2, 3)]
    drain()
    take_columns(m_top, 32, qh_top.at[c], 2, 32, 32)
    take_columns(m_top, 32, qh_top.at[c], 3, 32, 32)
    in_qh = swap(qh_top.at[c], qh_top)
    all_of(in_qg)
    all_of(in_pg)
    update_mid.finish()
    top = (pg_top[...].reshape(256, HALF) - dot(qg_top[...].reshape(256, 2048), whole(d_um))).astype(BF16)
    d_st[:, y, x] = top.reshape(4, 64, HALF)

    top_rows = Gather(d_st)
    top_rows.begin()
    spread_columns(b_low, c_low.at[c], 0, 128, 32)
    in_c_low = swap(c_low.at[c], c_low)
    top_rows.forward(0, 1, 3, 2)
    o_st[...] = d_st[z4, y, x].reshape(2, 32, HALF)
    give(solved_top, o_st)
    in_qh()
    o_ht[...] = (ph_top[...] - dot(qh_top[...].reshape(64, 2048), whole(d_um)).reshape(2, 32, HALF)).astype(BF16)
    give(half_top, o_ht)
    drain()
    in_g_mid()
    all_of(in_c_mid)
    top_rows.finish()
    mid = (g_mid[...].reshape(256, HALF) - dot(c_mid[...].reshape(256, 4096), whole(d_st))).astype(BF16)
    d_sm[:, y, x] = mid.reshape(2, 128, HALF)
    mid_rows = Gather(d_sm)
    mid_rows.begin()
    mid_rows.forward(0, 1, 3, 2)
    o_sm[...] = d_sm[z2, y, x].reshape(2, 64, HALF)
    give(solved_mid, o_sm)
    for copy, wait in given:
        copy.wait()
        wait()
    n_given = len(given)
    in_c_low()
    drain()
    mid_rows.finish()
    result = acc_low[...] - dot(c_low[...].reshape(256, 4096), whole(d_sm)).reshape(2, 128, HALF)
    o_sl[...] = result.astype(BF16)
    give(solved_low, o_sl)
    for copy, wait in given[n_given:]:
        copy.wait()
        wait()
    drain()


def hand_over(*refs):
    ins, outs, held, sems = refs[:6], refs[6:12], refs[12:18], refs[18]
    first = [pltpu.make_async_copy(a, b, sems.at[i, 0]) for i, (a, b) in enumerate(zip(ins, held))]
    second = [pltpu.make_async_copy(a, b, sems.at[i, 1]) for i, (a, b) in enumerate(zip(held, outs))]
    for copy in first:
        copy.start()
    for one, two in zip(first, second):
        one.wait()
        two.start()
    for copy in second:
        copy.wait()


def body(*args):
    shapes = (128, 64, 32, 128, 64, 32)

    def vmem(*shape, dtype=BF16):
        return pltpu.VMEM(shape, dtype)

    results = tuple(jax.ShapeDtypeStruct((1, n, 256), BF16) for n in shapes)
    anywhere = pl.BlockSpec(memory_space=pl.ANY)
    found = pl.pallas_call(
        kernel,
        out_shape=results,
        in_specs=[anywhere] * 15,
        out_specs=(anywhere,) * 6,
        scratch_shapes=[
            vmem(1, 4, 4, 256, HALF), vmem(2, 4, 4, 64, HALF), vmem(4, 4, 4, 32, HALF), vmem(4, 4, 4, 64, HALF),
            vmem(2, 4, 4, 128, HALF), vmem(2, 4, 4, 128, HALF), vmem(4, 4, 4, 64, HALF),
            vmem(2, 32, 4096), vmem(2, 2, 128, 4096), vmem(2, 144, 4096), vmem(2, 64, 4096),
            vmem(128, 1024), vmem(2, 64, 1024),
            vmem(16, 1024, dtype=jnp.int32), vmem(8, 1024, dtype=jnp.int32),
            vmem(4, 256, 1024), vmem(2, 1024, 256), vmem(8, 1024, dtype=jnp.int32),
            vmem(2, 144, 2048), vmem(4, 2, 32, 2048), vmem(2, 32, 2048), vmem(2, 128, 4096), vmem(2, 2, 64, 4096),
            vmem(2, 128, HALF, dtype=F32), vmem(2, 144, HALF, dtype=F32), vmem(2, 2, 64, HALF, dtype=F32),
            vmem(4, 2, 32, HALF, dtype=F32), vmem(2, 32, HALF, dtype=F32),
            vmem(2, 128, HALF), vmem(2, 64, HALF), vmem(2, 32, HALF),
            vmem(2, 128, HALF), vmem(2, 64, HALF), vmem(2, 32, HALF),
            pltpu.SemaphoreType.DMA((15,)), pltpu.SemaphoreType.DMA((6,)),
            pltpu.SemaphoreType.DMA((COPIES,)), pltpu.SemaphoreType.DMA((COPIES,)),
        ],
        compiler_params=pltpu.CompilerParams(
            collective_id=0, has_side_effects=True, vmem_limit_bytes=56 << 20
        ),
        cost_estimate=pl.CostEstimate(flops=7 * 10**9, bytes_accessed=10 << 20, transcendentals=0),
        name="sweeps",
    )(*args)
    return pl.pallas_call(
        hand_over,
        out_shape=results,
        in_specs=[anywhere] * 6,
        out_specs=(anywhere,) * 6,
        scratch_shapes=[vmem(1, n, 256) for n in shapes] + [pltpu.SemaphoreType.DMA((6, 2))],
        name="hand_over",
    )(*found)


def solution(mesh):
    split = P("leaf", "panel", None)
    return jax.shard_map(
        body,
        mesh=mesh,
        in_specs=(split,) * 13 + (P(), P()),
        out_specs=(split,) * 6,
        check_vma=False,
    )
```

```python
import jax
import jax.numpy as jnp
from jax import lax
from jax.experimental import pallas as pl
from jax.experimental.pallas import tpu as pltpu
from jax.sharding import PartitionSpec as P

MESH = pl.DeviceIdType.MESH
BF16, F32 = jnp.bfloat16, jnp.float32
HALF = 128
COPIES = 192


def kernel(
    probe_low, probe_mid, probe_top, inv_low, inv_mid, inv_top, gram_low, gram_mid, gram_top,
    panel_low, panel_mid, back_low, back_mid, sep_low, sep_mid,
    half_low, half_mid, half_top, solved_low, solved_mid, solved_top,
    d_rl, d_ul, d_um, d_st, d_sm, d_pm, d_pt,
    m_pl, m_low, m_mid, m_top, b_low, b_mid, s_low, s_mid, onehot, onehot_t, high,
    q_mid, qg_top, qh_top, c_low, c_mid, acc_low, acc_mid, g_mid, pg_top, ph_top,
    o_hl, o_hm, o_ht, o_sl, o_sm, o_st,
    load_sem, out_sem, send_sem, recv_sem,
):
    z = lax.axis_index("leaf")
    p = lax.axis_index("panel")
    c = lax.rem(p, 2)
    x = lax.rem(p // 2, 4)
    y = p // 8
    z2, z4 = lax.rem(z, 2), lax.rem(z, 4)
    cols = pl.ds(pl.multiple_of(c * HALF, HALF), HALF)
    other_cols = pl.ds(pl.multiple_of((1 - c) * HALF, HALF), HALF)

    def place(d, e, core=c):
        return x ^ jnp.where(core == 0, d, e), y ^ jnp.where(core == 0, e, d)

    def device(d=0, e=0, dz=0, core=c):
        xx, yy = place(d, e, core)
        return {"leaf": z ^ dz, "panel": (yy * 4 + xx) * 2 + core}

    sibling = {"leaf": z, "panel": p + 1 - 2 * c}

    def rows(count):
        return pl.ds(pl.multiple_of(c * count, count), count)

    def other(count):
        return pl.ds(pl.multiple_of((1 - c) * count, count), count)

    n_loads = [0]

    def load(src, dst):
        copy = pltpu.make_async_copy(src, dst, load_sem.at[n_loads[0]])
        n_loads[0] += 1
        copy.start()
        return copy

    own = [
        load(probe_low.at[0, :, cols], d_rl.at[0, y, x, rows(128)]),
        load(probe_mid.at[0, :, cols], d_pm.at[z2, y, x, rows(64)]),
        load(probe_top.at[0, :, cols], d_pt.at[z4, y, x, rows(32)]),
    ]
    load_sep = [load(sep_low, s_low), load(sep_mid, s_mid)]
    load_mid = [
        load(panel_mid.at[0], m_mid.at[c, 0:16]),
        load(inv_mid.at[0], m_mid.at[c, 16:80]),
        load(gram_mid.at[0], m_mid.at[c, 80:144]),
    ]
    load_top = [load(gram_top.at[0], m_top.at[c, 0:32]), load(inv_top.at[0], m_top.at[c, 32:64])]
    load_pl = load(panel_low.at[0], m_pl.at[c])
    load_back = [load(back_low.at[0], b_low), load(back_mid.at[0], b_mid.at[z2])]
    load_low = [load(inv_low.at[0], m_low.at[c, 0]), load(gram_low.at[0], m_low.at[c, 1])]

    barrier = pltpu.get_barrier_semaphore()
    partners = [sibling]
    for d in (1, 2, 3):
        partners += [device(d), device(0, d), device(dz=d), device(d, dz=1)]
        partners += [device(d, core=1 - c), device(0, d, core=1 - c)]
    for partner in partners:
        pl.semaphore_signal(barrier, 1, device_id=partner, device_id_type=MESH)
    pl.semaphore_wait(barrier, len(partners))

    n_sent = [0]
    unsent = []

    def send(src, dst, to, arriving=None):
        i = n_sent[0]
        n_sent[0] += 1
        copy = pltpu.make_async_remote_copy(
            src, dst, send_sem.at[i], recv_sem.at[i], device_id=to, device_id_type=MESH
        )
        copy.start()
        unsent.append(copy)
        if arriving is None:
            arriving = dst

        def wait():
            pltpu.make_async_remote_copy(
                arriving, arriving, send_sem.at[i], recv_sem.at[i], device_id=to, device_id_type=MESH
            ).wait_recv()

        return wait

    def drain():
        for copy in unsent:
            copy.wait_send()
        unsent.clear()

    def all_of(waits):
        for wait in waits:
            wait()

    def swap(src, buf, *at):
        return send(src, buf.at[(c, *at)], sibling, buf.at[(1 - c, *at)])

    def swap_probe(src, buf, zz, n):
        return send(
            src.at[0, :, other_cols], buf.at[zz, y, x, rows(n)], sibling, buf.at[zz, y, x, other(n)]
        )

    class Gather:
        def __init__(self, buf):
            self.buf, self.first, self.second = buf, {1: [], 2: [], 3: [], 0: []}, []

        def part(self, d, e, zz=slice(None)):
            xx, yy = place(d, e)
            return self.buf.at[zz, yy, xx]

        def begin(self, zz=slice(None)):
            for d in (1, 3, 2):
                self.first[d].append(
                    send(self.part(0, 0, zz), self.part(0, 0, zz), device(d), self.part(d, 0, zz))
                )

        def begin_pair(self):
            here, there = z2, 1 - z2
            for d, dz in ((1, 0), (3, 0), (0, 1), (1, 1), (3, 1), (2, 0), (2, 1)):
                self.first[d].append(
                    send(
                        self.part(0, 0, here), self.part(0, 0, here), device(d, dz=dz),
                        self.part(d, 0, there if dz else here),
                    )
                )

        def planes(self, offsets, here):
            self.z = [
                (here ^ d, send(self.part(0, 0, here), self.part(0, 0, here), device(dz=d), self.part(0, 0, here ^ d)))
                for d in offsets
            ]

        def relay(self):
            for zz, wait in self.z:
                wait()
                for d in (1, 3, 2):
                    self.first[d].append(
                        send(self.part(0, 0, zz), self.part(0, 0, zz), device(d), self.part(d, 0, zz))
                    )

        def forward(self, *offsets):
            for d in offsets:
                all_of(self.first[d])
                for e in (1, 3, 2):
                    self.second.append(
                        send(self.part(d, 0), self.part(d, 0), device(0, e), self.part(d, e))
                    )

        def finish(self):
            all_of(self.second)

    def dot(a, b):
        return jnp.dot(a, b, preferred_element_type=F32)

    def whole(buf):
        return buf[...].reshape(-1, HALF)

    def tables(first, count):
        for i in range(first, first + count):
            table, row = (s_low, (z - z2) + i) if i < 2 else (s_mid, 2 * (z // 4) + i - 2)
            sep = table[pl.ds(row, 1), :]
            high[i : i + 1, :] = lax.shift_right_logical(sep, 8)
            low = jnp.bitwise_and(sep, 255)
            for j in range(4):
                at = slice(j * 256, (j + 1) * 256)
                grid = lax.broadcasted_iota(jnp.int32, (256, 256), 0)
                hot = jnp.where(grid == low[:, at], 1.0, 0.0)
                onehot[i, :, at] = hot.astype(BF16)

    def own_tables():
        for i, (table, row) in enumerate(((s_low, z), (s_mid, z // 2))):
            sep = table[pl.ds(row, 1), :]
            high[4 + i : 5 + i, :] = lax.shift_right_logical(sep, 8)
            low = jnp.bitwise_and(sep, 255)
            for j in range(4):
                at = slice(j * 256, (j + 1) * 256)
                grid = lax.broadcasted_iota(jnp.int32, (256, 256), 0)
                hot = jnp.where(grid == low[:, at], 1.0, 0.0)
                onehot_t[i, at, :] = hot.T.astype(BF16)

    def take_columns(src, start, dst, i, total, block):
        at0 = (i % 2) * 1024

        def step(r, _):
            value = src[c, pl.ds(pl.multiple_of(start + r * block, 16), block), :]
            tall = jnp.concatenate([value[:, k * 256 : (k + 1) * 256] for k in range(16)], 0)
            part = pl.ds(pl.multiple_of(r * block, 16), block)
            for j in range(4):
                at = slice(j * 256, (j + 1) * 256)
                found = dot(tall, onehot[i, :, at])
                which = high[i : i + 1, at]
                picked = jnp.zeros((block, 256), F32)
                for k in range(16):
                    picked = jnp.where(which == k, found[k * block : (k + 1) * block], picked)
                dst[part, at0 + j * 256 : at0 + (j + 1) * 256] = picked.astype(BF16)
            return 0

        lax.fori_loop(0, total // block, step, 0)

    def spread_columns(src, dst, i, total, block):
        def step(r, _):
            part = pl.ds(pl.multiple_of(r * block, block), block)
            value = src[part, :]
            which = high[4 + i : 5 + i, :]
            tall = jnp.concatenate(
                [value * jnp.where(which == k, 1.0, 0.0).astype(BF16) for k in range(16)], 0
            )
            found = dot(tall, onehot_t[i])
            for k in range(16):
                dst[part, k * 256 : (k + 1) * 256] = found[k * block : (k + 1) * block].astype(BF16)
            return 0

        lax.fori_loop(0, total // block, step, 0)

    given = []

    def give(out, buf):
        copy = pltpu.make_async_copy(buf.at[c], out.at[0, :, cols], out_sem.at[len(given)])
        copy.start()
        given.append((copy, send(buf.at[1 - c], out.at[0, :, cols], sibling, out.at[0, :, other_cols])))

    right_low = Gather(d_rl)
    mine = d_rl.at[0, y, x, rows(128)]
    for d in (1, 3, 2):
        xx, yy = place(d, 0)
        right_low.first[d].append(
            send(probe_low.at[0, :, cols], mine, device(d), d_rl.at[0, yy, xx, rows(128)])
        )
        right_low.first[d].append(
            send(probe_low.at[0, :, other_cols], mine, device(d, core=1 - c), d_rl.at[0, yy, xx, other(128)])
        )
    right_low.first[0].append(swap_probe(probe_low, d_rl, 0, 128))
    in_pm = swap_probe(probe_mid, d_pm, z2, 64)
    in_pt = swap_probe(probe_top, d_pt, z4, 32)
    in_back = send(back_mid.at[0], b_mid.at[z2], device(dz=1), b_mid.at[1 - z2])
    own[1].wait()
    in_pm()
    pm = Gather(d_pm)
    pm.planes((1,), z2)
    pm.begin(z2)
    own[2].wait()
    in_pt()
    pt = Gather(d_pt)
    pt.planes((1, 2, 3), z4)
    own[0].wait()
    right_low.forward(0)
    in_pl = swap(panel_low.at[0], m_pl)
    all_of([copy.wait for copy in load_sep])
    tables(2, 2)
    all_of([copy.wait for copy in load_top])
    take_columns(m_top, 0, qg_top.at[z4, c], 2, 32, 32)
    take_columns(m_top, 0, qg_top.at[z4, c], 3, 32, 32)
    piece = qg_top.at[z4, c]
    z_qg = [(d, send(piece, piece, device(dz=d), qg_top.at[z4 ^ d, c])) for d in (1, 2, 3)]
    right_low.forward(1, 3, 2)
    pm.relay()
    in_qg = [send(piece, piece, sibling, qg_top.at[z4, 1 - c])]
    in_mid = [
        swap(panel_mid.at[0], m_mid, slice(0, 16)),
        swap(inv_mid.at[0], m_mid, slice(16, 80)),
        swap(gram_mid.at[0], m_mid, slice(80, 144)),
    ]
    in_low = [swap(inv_low.at[0], m_low, 0), swap(gram_low.at[0], m_low, 1)]
    in_top = [swap(gram_top.at[0], m_top, slice(0, 32)), swap(inv_top.at[0], m_top, slice(32, 64))]
    tables(0, 2)
    all_of([copy.wait for copy in load_mid])
    take_columns(m_mid, 0, q_mid.at[c], 0, 144, 48)
    take_columns(m_mid, 0, q_mid.at[c], 1, 144, 48)
    in_q_mid = swap(q_mid.at[c], q_mid)
    pm.forward(0, 1, 3, 2)
    load_pl.wait()
    in_pl()
    update = jnp.zeros((64, HALF), F32)
    for k, d in enumerate((0, 1, 3, 2)):
        all_of(right_low.second[3 * k : 3 * k + 3])
        for e in range(4):
            xx, yy = place(d, e)
            at = pl.ds(pl.multiple_of((yy * 4 + xx) * 256, 256), 256)
            update += dot(m_pl[:, :, at].reshape(64, 256), d_rl[0, yy, xx])
    d_ul[z2, y, x] = update.astype(BF16)

    update_low = Gather(d_ul)
    update_low.begin_pair()
    pt.begin(z4)
    pt.relay()
    own_tables()
    all_of([copy.wait for copy in load_back])
    in_back()
    spread_columns(b_mid.at[z2], c_mid.at[z2, c], 1, 64, 32)
    update_low.forward(0, 1, 3, 2)
    spread_columns(b_mid.at[1 - z2], c_mid.at[1 - z2, c], 1, 64, 32)
    in_c_mid = [
        send(c_mid.at[zz, c], c_mid.at[zz, c], sibling, c_mid.at[zz, 1 - c]) for zz in (0, 1)
    ]
    drain()
    all_of(in_mid)
    pm.finish()
    acc_mid[...] = dot(m_mid[...].reshape(288, 4096), whole(d_pm)).reshape(2, 144, HALF)
    in_q_mid()
    pt.forward(0, 1, 3, 2)
    update_low.finish()
    update = acc_mid[:, 0:16].reshape(32, HALF) - dot(q_mid[:, 0:16].reshape(32, 2048), whole(d_ul))
    d_um[z4, y, x] = update.astype(BF16)

    update_mid = Gather(d_um)
    update_mid.planes((1, 2, 3), z4)
    update_mid.begin(z4)
    result = acc_mid[:, 16:144] - dot(q_mid[:, 16:144].reshape(256, 2048), whole(d_ul)).reshape(2, 128, HALF)
    o_hm[...] = result[:, 0:64].astype(BF16)
    g_mid[z2] = result[:, 64:128]
    update_mid.relay()
    in_g_mid = send(g_mid.at[z2], g_mid.at[z2], device(dz=1), g_mid.at[1 - z2])
    give(half_mid, o_hm)
    for d, wait in z_qg:
        wait()
        piece = qg_top.at[z4 ^ d, c]
        in_qg.append(send(piece, piece, sibling, qg_top.at[z4 ^ d, 1 - c]))
    all_of([copy.wait for copy in load_low])
    all_of(in_low)
    result = dot(m_low[...].reshape(512, 4096), whole(d_rl)).reshape(2, 2, 128, HALF)
    o_hl[...] = result[:, 0].astype(BF16)
    acc_low[...] = result[:, 1]
    update_mid.forward(0, 1, 3, 2)
    give(half_low, o_hl)
    all_of(in_top)
    pt.finish()
    result = dot(m_top[...].reshape(128, 4096), whole(d_pt)).reshape(2, 64, HALF)
    pg_top[z4] = result[:, 0:32]
    ph_top[...] = result[:, 32:64]
    in_pg = [send(pg_top.at[z4], pg_top.at[z4], device(dz=d), pg_top.at[z4 ^ d]) for d in (1, 2, 3)]
    drain()
    take_columns(m_top, 32, qh_top.at[c], 2, 32, 32)
    take_columns(m_top, 32, qh_top.at[c], 3, 32, 32)
    in_qh = swap(qh_top.at[c], qh_top)
    all_of(in_qg)
    all_of(in_pg)
    update_mid.finish()
    top = (pg_top[...].reshape(256, HALF) - dot(qg_top[...].reshape(256, 2048), whole(d_um))).astype(BF16)
    d_st[:, y, x] = top.reshape(4, 64, HALF)

    top_rows = Gather(d_st)
    top_rows.begin()
    spread_columns(b_low, c_low.at[c], 0, 128, 32)
    in_c_low = swap(c_low.at[c], c_low)
    top_rows.forward(0, 1, 3, 2)
    o_st[...] = d_st[z4, y, x].reshape(2, 32, HALF)
    give(solved_top, o_st)
    in_qh()
    o_ht[...] = (ph_top[...] - dot(qh_top[...].reshape(64, 2048), whole(d_um)).reshape(2, 32, HALF)).astype(BF16)
    give(half_top, o_ht)
    drain()
    in_g_mid()
    all_of(in_c_mid)
    top_rows.finish()
    mid = (g_mid[...].reshape(256, HALF) - dot(c_mid[...].reshape(256, 4096), whole(d_st))).astype(BF16)
    d_sm[:, y, x] = mid.reshape(2, 128, HALF)
    mid_rows = Gather(d_sm)
    mid_rows.begin()
    mid_rows.forward(0, 1, 3, 2)
    o_sm[...] = d_sm[z2, y, x].reshape(2, 64, HALF)
    give(solved_mid, o_sm)
    for copy, wait in given:
        copy.wait()
        wait()
    n_given = len(given)
    in_c_low()
    drain()
    mid_rows.finish()
    result = acc_low[...] - dot(c_low[...].reshape(256, 4096), whole(d_sm)).reshape(2, 128, HALF)
    o_sl[...] = result.astype(BF16)
    give(solved_low, o_sl)
    for copy, wait in given[n_given:]:
        copy.wait()
        wait()
    drain()


def hand_over(*refs):
    ins, outs, held, sems = refs[:6], refs[6:12], refs[12:18], refs[18]
    first = [pltpu.make_async_copy(a, b, sems.at[i, 0]) for i, (a, b) in enumerate(zip(ins, held))]
    second = [pltpu.make_async_copy(a, b, sems.at[i, 1]) for i, (a, b) in enumerate(zip(held, outs))]
    for copy in first:
        copy.start()
    for one, two in zip(first, second):
        one.wait()
        two.start()
    for copy in second:
        copy.wait()


def body(*args):
    shapes = (128, 64, 32, 128, 64, 32)

    def vmem(*shape, dtype=BF16):
        return pltpu.VMEM(shape, dtype)

    results = tuple(jax.ShapeDtypeStruct((1, n, 256), BF16) for n in shapes)
    anywhere = pl.BlockSpec(memory_space=pl.ANY)
    found = pl.pallas_call(
        kernel,
        out_shape=results,
        in_specs=[anywhere] * 15,
        out_specs=(anywhere,) * 6,
        scratch_shapes=[
            vmem(1, 4, 4, 256, HALF), vmem(2, 4, 4, 64, HALF), vmem(4, 4, 4, 32, HALF), vmem(4, 4, 4, 64, HALF),
            vmem(2, 4, 4, 128, HALF), vmem(2, 4, 4, 128, HALF), vmem(4, 4, 4, 64, HALF),
            vmem(2, 32, 4096), vmem(2, 2, 128, 4096), vmem(2, 144, 4096), vmem(2, 64, 4096),
            vmem(128, 1024), vmem(2, 64, 1024),
            vmem(16, 1024, dtype=jnp.int32), vmem(8, 1024, dtype=jnp.int32),
            vmem(4, 256, 1024), vmem(2, 1024, 256), vmem(8, 1024, dtype=jnp.int32),
            vmem(2, 144, 2048), vmem(4, 2, 32, 2048), vmem(2, 32, 2048), vmem(2, 128, 4096), vmem(2, 2, 64, 4096),
            vmem(2, 128, HALF, dtype=F32), vmem(2, 144, HALF, dtype=F32), vmem(2, 2, 64, HALF, dtype=F32),
            vmem(4, 2, 32, HALF, dtype=F32), vmem(2, 32, HALF, dtype=F32),
            vmem(2, 128, HALF), vmem(2, 64, HALF), vmem(2, 32, HALF),
            vmem(2, 128, HALF), vmem(2, 64, HALF), vmem(2, 32, HALF),
            pltpu.SemaphoreType.DMA((15,)), pltpu.SemaphoreType.DMA((6,)),
            pltpu.SemaphoreType.DMA((COPIES,)), pltpu.SemaphoreType.DMA((COPIES,)),
        ],
        compiler_params=pltpu.CompilerParams(
            collective_id=0, has_side_effects=True, vmem_limit_bytes=56 << 20
        ),
        cost_estimate=pl.CostEstimate(flops=7 * 10**9, bytes_accessed=10 << 20, transcendentals=0),
        name="sweeps",
    )(*args)
    return pl.pallas_call(
        hand_over,
        out_shape=results,
        in_specs=[anywhere] * 6,
        out_specs=(anywhere,) * 6,
        scratch_shapes=[vmem(1, n, 256) for n in shapes] + [pltpu.SemaphoreType.DMA((6, 2))],
        name="hand_over",
    )(*found)


def solution(mesh):
    split = P("leaf", "panel", None)
    return jax.shard_map(
        body,
        mesh=mesh,
        in_specs=(split,) * 13 + (P(), P()),
        out_specs=(split,) * 6,
        check_vma=False,
    )
```
